32 devices in a mesh: ctx: 8 (over z, x), rep: 4 (over y, core).
Axes of the slice: x: 2, y: 2, z: 4, core: 2. Of those that a mesh axis runs over, the one named last changes fastest.
Arguments:
- query: bfloat16 [4096, 2048], P(('rep', 'ctx')), parts along dimension 0, may hold values from -6 to 6
- key: bfloat16 [4096, 2048], P(('rep', 'ctx')), parts along dimension 0, may hold values from -6 to 6
- value: bfloat16 [4096, 2048], P(('rep', 'ctx')), parts along dimension 0, may hold values from -6 to 6
- beta: float32 [4096, 16], P(('rep', 'ctx')), parts along dimension 0, may hold values from 0.05 to 0.95
- log_gate: float32 [4096, 16], P(('rep', 'ctx')), parts along dimension 0, may hold values from -1.5 to 0
- level_weight: float32 [4096, 16, 4], P(('rep', 'ctx')), parts along dimension 0, may hold values from 0.1 to 1.5
- norm_gain: float32 [128], replicated, may hold values from 0.5 to 1.5
- grad_out: bfloat16 [4096, 2048], P(('rep', 'ctx')), parts along dimension 0, may hold values from -6 to 6
- grad_final_state: float32 [8192, 128], P(('rep', 'ctx')), parts along dimension 0, may hold values from -6 to 6
Outputs:
- grad_query: bfloat16 [4096, 2048], P(('rep', 'ctx')), parts along dimension 0
- grad_key: bfloat16 [4096, 2048], P(('rep', 'ctx')), parts along dimension 0
- grad_value: bfloat16 [4096, 2048], P(('rep', 'ctx')), parts along dimension 0
- grad_beta: float32 [4096, 16], P(('rep', 'ctx')), parts along dimension 0
- grad_level: float32 [4096, 16, 4], P(('rep', 'ctx')), parts along dimension 0
- grad_gain: float32 [512], P('rep'), parts along dimension 0
- final_state: float32 [8192, 128], P(('rep', 'ctx')), parts along dimension 0
The draws below stay inside these ranges and needn't reach their ends.
There are 4 independent parts, one for each index of `rep`. The reference program is written for one: setup_inputs(seed, part) draws one part's arguments, and reference() takes and returns one part's arrays. A program takes and returns all parts, laid end to end along the dimension named above; an argument that names none is the same for every part. Nothing has to cross between parts.
All inputs are finite; a program needn't handle non-finite values.
Results may differ from the reference program's by a relative error of at most 0.001.
Values sent between devices are 32-bit elements; how exact they have to be, the bound alone decides.
A program may use at most 128 MiB of HBM per device.

```python
import jax
import jax.numpy as jnp
from jax import lax

HEAD_TOTAL = 16
DK = 128
DV = 128
TOK_DEV = 128
SEQUENCE_TOKENS = 1024
LEVELS = 4
N_CTX = 8


def draw_log_gate(key, part):
    base_key = jax.random.fold_in(key, 11)
    key_sequence = jax.random.split(base_key, 7)
    fast_share = 0.5
    is_fast = jax.random.uniform(key_sequence[0], (HEAD_TOTAL,)) < fast_share
    fast_rate = 1.0 / jax.random.uniform(key_sequence[1], (HEAD_TOTAL,), minval=30.0, maxval=50.0)
    slow_rate = jnp.exp(jax.random.uniform(key_sequence[2], (HEAD_TOTAL,), minval=jnp.log(0.05), maxval=jnp.log(0.3))) / SEQUENCE_TOKENS
    head_rates = jnp.where(is_fast, fast_rate, slow_rate)
    block_factor = jnp.exp(jax.random.uniform(key_sequence[3], (SEQUENCE_TOKENS // TOK_DEV, HEAD_TOTAL), minval=-0.7, maxval=0.7))
    block_factor = jnp.repeat(block_factor, TOK_DEV, axis=0)
    token_factor = jax.random.uniform(key_sequence[4], (SEQUENCE_TOKENS, HEAD_TOTAL), minval=0.5, maxval=1.5)
    gate_logarithms = -head_rates[None, :] * block_factor * token_factor
    flush_position = jax.random.randint(key_sequence[5], (2, HEAD_TOTAL), 0, SEQUENCE_TOKENS)
    flush_keep_mask = jax.random.uniform(key_sequence[6], (2, HEAD_TOTAL), minval=0.5, maxval=0.8)
    token_positions = jnp.arange(SEQUENCE_TOKENS, dtype=jnp.int32)
    match_mask = token_positions[None, :, None] == flush_position[:, None, :]
    gate_logarithms = gate_logarithms + jnp.sum(jnp.where(match_mask, jnp.log(flush_keep_mask)[:, None, :], 0.0), axis=0)
    return gate_logarithms.astype(jnp.float32)


def draw_key(key, part):
    base_key = jax.random.fold_in(key, 23)
    key_sequence = jax.random.split(base_key, 3)
    block_count = SEQUENCE_TOKENS // TOK_DEV
    pair_count = block_count * HEAD_TOTAL
    ranking = jax.random.permutation(key_sequence[0], pair_count)
    aligned = (ranking < pair_count // 2).reshape(block_count, 1, HEAD_TOTAL, 1)
    direction = jax.random.normal(key_sequence[1], (block_count, 1, HEAD_TOTAL, DK), dtype=jnp.float32)
    noise = jax.random.normal(key_sequence[2], (block_count, TOK_DEV, HEAD_TOTAL, DK), dtype=jnp.float32)
    strength = 2.5
    entries = noise + jnp.where(aligned, strength * direction, 0.0)
    entries = jnp.clip(entries, -6.0, 6.0)
    return entries.reshape(SEQUENCE_TOKENS, HEAD_TOTAL * DK).astype(jnp.bfloat16)


def level_of(stream_key, dims, pieces, smallest, top_value):
    level = 1.0
    for position, parts in pieces:
        steps = jax.random.uniform(jax.random.fold_in(jax.random.fold_in(stream_key, 6), position), (parts,), jnp.float32, smallest / len(pieces), top_value / len(pieces))
        level = level * jnp.repeat(jnp.exp(steps), dims[position] // parts).reshape((-1,) + (1,) * (len(dims) - 1 - position))
    return level


def bell_draw(stream_key, shape, spread, most, cuts=(), kind=jnp.bfloat16):
    result = spread * jax.random.normal(stream_key, shape, jnp.float32)
    if cuts:
        result = result * level_of(stream_key, shape, cuts, -0.22, 0.18)
    return jnp.clip(result, -most, most).astype(kind)


def setup_inputs(seed: int = 0, part: int = 0) -> dict:
    keys = jax.random.split(jax.random.key(seed), 10)
    part_keys = jax.random.split(jax.random.fold_in(keys[9], part), 10)
    query = bell_draw(part_keys[0], (SEQUENCE_TOKENS, HEAD_TOTAL * DK), 1.0, 6.0, ((0, 8),))
    key = draw_key(jax.random.fold_in(jax.random.fold_in(keys[9], part), 71), part)
    value = bell_draw(part_keys[2], (SEQUENCE_TOKENS, HEAD_TOTAL * DV), 1.0, 6.0, ((0, 8),))
    beta = jnp.clip(0.05 + 0.9 * jax.random.uniform(part_keys[3], (SEQUENCE_TOKENS, HEAD_TOTAL), jnp.float32) ** level_of(part_keys[3], (SEQUENCE_TOKENS, HEAD_TOTAL), ((0, 8),), -0.2, 0.2), 0.05, 0.95)
    log_gate = draw_log_gate(jax.random.fold_in(jax.random.fold_in(keys[9], part), 71), part)
    level_weight = jnp.clip(0.1 + 1.4 * jax.random.uniform(part_keys[5], (SEQUENCE_TOKENS, HEAD_TOTAL, LEVELS), jnp.float32) ** level_of(part_keys[5], (SEQUENCE_TOKENS, HEAD_TOTAL, LEVELS), ((0, 8),), -0.2, 0.2), 0.1, 1.5)
    norm_gain = jnp.clip(1.0 + 0.1 * jax.random.normal(keys[6], (DV,), jnp.float32), 0.5, 1.5)
    grad_out = bell_draw(part_keys[7], (SEQUENCE_TOKENS, HEAD_TOTAL * DV), 1.0, 6.0, ((0, 8),))
    grad_final_state = bell_draw(part_keys[8], (HEAD_TOTAL * DK, DV), 1.0, 6.0, ((0, 8),), jnp.float32)
    return dict(query=query, key=key, value=value, beta=beta, log_gate=log_gate, level_weight=level_weight, norm_gain=norm_gain, grad_out=grad_out, grad_final_state=grad_final_state)


epsilon = 1e-06
topmost_level = lax.Precision.HIGHEST

def normalize(values):
    return values * lax.rsqrt(lax.optimization_barrier(jnp.sum(values * values, axis=-1, keepdims=True)) + epsilon)

def split_heads(values, head_count):
    row_count = values.shape[0]
    return values.reshape(row_count, head_count, -1).transpose(1, 0, 2)

def prepare(query, key, value, beta, cum_gate):
    head_count = cum_gate.shape[0]
    row_count = cum_gate.shape[1]
    query_normed = normalize(split_heads(query, head_count))
    normalized_key = normalize(split_heads(key, head_count))
    value_heads = split_heads(value, head_count)
    beta_heads = beta.T
    strict = jnp.tril(jnp.ones((row_count, row_count), dtype=bool), -1)
    log_gaps = cum_gate[:, :, None] - cum_gate[:, None, :]
    decays = jnp.exp(jnp.where(strict[None], log_gaps, -jnp.inf))
    key_inner = jnp.einsum('htk,hsk->hts', normalized_key, normalized_key, precision=topmost_level)
    system = jnp.eye(row_count, dtype=cum_gate.dtype)[None] + beta_heads[:, :, None] * decays * key_inner
    surrogate_value = jax.scipy.linalg.solve_triangular(system, beta_heads[:, :, None] * value_heads, lower=True)
    trailing_decay = jnp.exp(cum_gate[:, -1:] - cum_gate)
    state_per_block = jnp.einsum('fni,fnb->fib', normalized_key * trailing_decay[:, :, None], surrogate_value, precision=topmost_level)
    return (query_normed, normalized_key, surrogate_value, state_per_block)

def finish(query_normed, normalized_key, surrogate_value, level_weight, norm_gain, bucket_states, cum_gate):
    row_count = cum_gate.shape[1]
    inclusive = jnp.tril(jnp.ones((row_count, row_count), dtype=bool))
    log_gaps = cum_gate[:, :, None] - cum_gate[:, None, :]
    decays = jnp.exp(jnp.where(inclusive[None], log_gaps, -jnp.inf))
    attention_scores = jnp.einsum('htk,hsk->hts', query_normed, normalized_key, precision=topmost_level) * decays
    intra_out = jnp.einsum('hts,hsv->htv', attention_scores, surrogate_value, precision=topmost_level)
    cross_out = jnp.einsum('htk,lhkv->lhtv', query_normed, bucket_states, precision=topmost_level)
    level_heads = level_weight.transpose(1, 0, 2)
    weighted = level_heads[:, :, 1:] * jnp.exp(cum_gate)[:, :, None]
    mixture = level_heads[:, :, 0:1] * intra_out + jnp.einsum('htl,lhtv->htv', weighted, cross_out, precision=topmost_level)
    inverse_rms = lax.rsqrt(lax.optimization_barrier(jnp.mean(mixture * mixture, axis=-1, keepdims=True)) + epsilon)
    normed = mixture * inverse_rms * norm_gain
    return normed.transpose(1, 0, 2).reshape(row_count, -1)

def reference(query, key, value, beta, log_gate, level_weight, norm_gain, grad_out, grad_final_state):
    blocks = N_CTX
    row_count = TOK_DEV
    cum_gates = jnp.cumsum(log_gate.reshape(blocks, row_count, HEAD_TOTAL).transpose(0, 2, 1), axis=2)
    totals = cum_gates[:, :, -1]
    block_ends = jnp.cumsum(totals, axis=0)
    starts = block_ends - totals
    closing_coefficients = jnp.exp(block_ends[-1:, :] - block_ends)
    block_ids = jnp.arange(blocks, dtype=jnp.int32)
    xor_ids = jnp.bitwise_xor(block_ids[:, None], block_ids[None, :])
    earlier = block_ids[None, :] < block_ids[:, None]
    gaps = jnp.where(earlier[:, :, None], starts[:, None, :] - block_ends[None, :, :], -jnp.inf)
    coeffs = jnp.exp(gaps)
    level_spans = 2 ** jnp.arange(LEVELS - 1, dtype=jnp.int32)
    member = (xor_ids[:, None, :] >= level_spans[None, :, None]) & (xor_ids[:, None, :] < 2 * level_spans[None, :, None])
    weights = member[:, :, :, None].astype(totals.dtype) * coeffs[:, None, :, :]

    def forward(query_float, key_float, value_float, beta_float, level_float, gain_float):
        inputs = (query_float.reshape(blocks, row_count, -1), key_float.reshape(blocks, row_count, -1), value_float.reshape(blocks, row_count, -1), beta_float.reshape(blocks, row_count, HEAD_TOTAL), cum_gates)
        query_normed, normalized_key, surrogate_value, per_block_state_list = lax.map(lambda packed: prepare(*packed), inputs)

        def finish_block(packed):
            query_block, key_block, pseudo_block, level_block, gate_block, weight_block = packed
            bucket_states = jnp.einsum('ljh,jhkv->lhkv', weight_block, per_block_state_list, precision=topmost_level)
            return finish(query_block, key_block, pseudo_block, level_block, gain_float, bucket_states, gate_block)
        results = lax.map(finish_block, (query_normed, normalized_key, surrogate_value, level_float.reshape(blocks, row_count, HEAD_TOTAL, LEVELS), cum_gates, weights))
        closing_value = jnp.einsum('re,recy->ecy', closing_coefficients, per_block_state_list, precision=topmost_level)
        return (results.reshape(blocks * row_count, -1), closing_value.reshape(HEAD_TOTAL * DK, DV))
    primals = (query.astype(jnp.float32), key.astype(jnp.float32), value.astype(jnp.float32), beta, level_weight, norm_gain)
    results, backward = jax.vjp(forward, *primals)
    grads = backward((grad_out.astype(jnp.float32), grad_final_state))
    return (grads[0].astype(jnp.bfloat16), grads[1].astype(jnp.bfloat16), grads[2].astype(jnp.bfloat16), grads[3], grads[4], grads[5], results[1])
```

```python
import functools

import jax
import jax.numpy as jnp
from jax import lax
from jax.experimental import pallas as pl
from jax.experimental.pallas import tpu as pltpu
from jax.sharding import PartitionSpec as P

epsilon = 1e-06
topmost_level = lax.Precision.HIGHEST
NN = (((1,), (0,)), ((), ()))
NT = (((1,), (1,)), ((), ()))
CHUNKS = 4
HEADS_STEP = 2
VMEM_LIMIT = 48 * 2**20


def from_partner(value, axis, bit):
    mask = 2**bit
    pairs = [(source, source ^ mask) for source in range(lax.axis_size(axis))]
    return lax.ppermute(value, axis, pairs)


def cut(x):
    high = x.astype(jnp.bfloat16)
    return high, (x - high.astype(jnp.float32)).astype(jnp.bfloat16)


def dot1(a, b, dims=NN):
    return lax.dot_general(a, b, dims, preferred_element_type=jnp.float32)


def dot3(a, b, dims=NN):
    left = jnp.concatenate([a[0], a[1], a[0]], axis=1)
    right = jnp.concatenate([b[0], b[0], b[1]], axis=0 if dims is NN else 1)
    return dot1(left, right, dims)


def dot2_right(a, b, dims=NN):
    left = jnp.concatenate([a[0], a[1]], axis=1)
    right = jnp.concatenate([b, b], axis=0 if dims is NN else 1)
    return dot1(left, right, dims)


def dot2_left(a, b, dims=NN):
    left = jnp.concatenate([a, a], axis=1)
    right = jnp.concatenate([b[0], b[1]], axis=0 if dims is NN else 1)
    return dot1(left, right, dims)


def column(values, lane):
    lanes = lax.broadcasted_iota(jnp.int32, values.shape, 1)
    return jnp.sum(jnp.where(lanes == lane, values, 0.0), axis=1, keepdims=True)


def inverse_norm(values):
    return lax.rsqrt(jnp.sum(values * values, axis=-1, keepdims=True) + epsilon)


def coordinates(rows):
    shape = (rows, rows)
    return lax.broadcasted_iota(jnp.int32, shape, 0), lax.broadcasted_iota(jnp.int32, shape, 1)


def decay_of(gate_column, gate_row, keep):
    return jnp.exp(jnp.where(keep, gate_column - gate_row, -jnp.inf))


def prepare_kernel(base, k_ref, v_ref, beta_ref, cc_ref, cr_ref, t_ref, u_ref, s_ref):
    rows = k_ref.shape[0]
    width = t_ref.shape[2]
    size = s_ref.shape[1]
    t_ids, s_ids = coordinates(rows)
    systems = []
    for i in range(t_ref.shape[0]):
        head = base + pl.program_id(0) * t_ref.shape[0] + i
        key = k_ref[:, i * size : (i + 1) * size]
        gate = column(cc_ref[...], head)
        beta = column(beta_ref[...], head)
        gate_row = cr_ref[pl.ds(head, 1), :]
        key_float = key.astype(jnp.float32)
        key_normed = key_float * inverse_norm(key_float)
        keys = cut(key_normed)
        inner = dot3(keys, keys, NT)
        systems.append(
            beta * decay_of(gate, gate_row, s_ids < t_ids) * inner
        )
        systems[-1] = (systems[-1], gate, beta, key_normed)
    inverses = []
    for system, _, _, _ in systems:
        first = jnp.where((t_ids ^ s_ids) == 1, system, 0.0)
        inverses.append(jnp.where(t_ids == s_ids, 1.0, 0.0) - first)
    span = 2
    while span < rows:
        gap = t_ids ^ s_ids
        keep = (gap >= span) & (gap < 2 * span)
        for i, (system, _, _, _) in enumerate(systems):
            parts = cut(inverses[i])
            mixed = dot3(cut(jnp.where(keep, system, 0.0)), parts)
            inverses[i] = inverses[i] - dot3(parts, cut(mixed))
        span *= 2
    for i, (_, gate, beta, key_normed) in enumerate(systems):
        value = v_ref[:, i * u_ref.shape[2] : (i + 1) * u_ref.shape[2]].astype(jnp.float32)
        pseudo = dot3(cut(inverses[i]), cut(beta * value))
        trailing = jnp.exp(gate[rows - 1 :, :] - gate)
        state = dot3(cut((key_normed * trailing).T), cut(pseudo))
        t_ref[i] = inverses[i]
        u_ref[i] = pseudo
        s_ref[i] = state


def finish_kernel(
    base, levels, q_ref, k_ref, go_ref, u_ref, cc_ref, cr_ref, w_ref, f_ref, gain_ref, *refs
):
    bucket_refs = refs[: levels - 1]
    gq_ref, dk_ref, du_ref, gl_ref, gg_ref = refs[levels - 1 : levels + 4]
    back_refs = refs[levels + 4 :]
    rows = q_ref.shape[0]
    size = dk_ref.shape[2]
    vsize = du_ref.shape[2]
    heads = du_ref.shape[0]
    t_ids, s_ids = coordinates(rows)

    @pl.when(pl.program_id(0) == 0)
    def _():
        gl_ref[...] = jnp.zeros_like(gl_ref)
        gg_ref[...] = jnp.zeros_like(gg_ref)

    level_lanes = lax.broadcasted_iota(jnp.int32, gl_ref.shape, 1)
    grad_level = jnp.zeros(gl_ref.shape, jnp.float32)
    grad_gain = jnp.zeros(gg_ref.shape, jnp.float32)
    for i in range(heads):
        head = base + pl.program_id(0) * heads + i
        query = q_ref[:, i * size : (i + 1) * size]
        key = k_ref[:, i * size : (i + 1) * size]
        grad_out = go_ref[:, i * vsize : (i + 1) * vsize].astype(jnp.float32)
        gate = column(cc_ref[...], head)
        gate_row = cr_ref[pl.ds(head, 1), :]
        query_float = query.astype(jnp.float32)
        key_float = key.astype(jnp.float32)
        query_scale = inverse_norm(query_float)
        query_normed = query_float * query_scale
        key_normed = key_float * inverse_norm(key_float)
        queries = cut(query_normed)
        keys = cut(key_normed)
        pseudo = cut(u_ref[i])
        decay = decay_of(gate, gate_row, s_ids <= t_ids)
        scores = dot3(queries, keys, NT) * decay
        intra = dot3(cut(scores), pseudo)
        weight0 = column(w_ref[...], head * levels)
        mixture = weight0 * intra
        weights, crosses, buckets = [], [], []
        for l in range(levels - 1):
            bucket = cut(bucket_refs[l][i])
            cross = dot3(queries, bucket)
            weight = column(w_ref[...], head * levels + 1 + l)
            mixture = mixture + weight * cross
            weights.append(weight)
            crosses.append(cross)
            buckets.append(bucket)
        scale = lax.rsqrt(jnp.mean(mixture * mixture, axis=-1, keepdims=True) + epsilon)
        unit = mixture * scale
        grad_gain = grad_gain + jnp.sum(grad_out * unit, axis=0, keepdims=True)
        grad_unit = grad_out * gain_ref[...]
        grad_mix = scale * (
            grad_unit - unit * jnp.mean(grad_unit * unit, axis=-1, keepdims=True)
        )
        part = jnp.sum(grad_mix * intra, axis=-1, keepdims=True)
        grad_level = grad_level + jnp.where(level_lanes == head * levels, part, 0.0)
        grad_intra = weight0 * grad_mix
        grad_intra_parts = cut(grad_intra)
        grad_scores = dot3(grad_intra_parts, pseudo, NT) * decay
        grad_query = dot3(cut(grad_scores), keys)
        dk_ref[i] = dot3(cut(grad_scores.T), queries)
        du_ref[i] = dot3(cut(scores.T), grad_intra_parts)
        query_turned = cut(query_normed.T)
        for l in range(levels - 1):
            lane = head * levels + 1 + l
            part = jnp.sum(grad_mix * crosses[l], axis=-1, keepdims=True)
            part = part * column(f_ref[...], lane)
            grad_level = grad_level + jnp.where(level_lanes == lane, part, 0.0)
            weighted = cut(weights[l] * grad_mix)
            grad_query = grad_query + dot3(weighted, buckets[l], NT)
            back_refs[l][i] = dot3(query_turned, weighted)
        along = jnp.sum(grad_query * query_normed, axis=-1, keepdims=True)
        grad_query = query_scale * (grad_query - query_normed * along)
        gq_ref[:, i * size : (i + 1) * size] = grad_query.astype(gq_ref.dtype)
    gl_ref[...] += grad_level
    gg_ref[...] += grad_gain


def back_kernel(
    base, k_ref, v_ref, beta_ref, cc_ref, cr_ref, t_ref, u_ref, dk_ref, du_ref, ds_ref,
    gk_ref, gv_ref, gb_ref,
):
    rows = k_ref.shape[0]
    size = dk_ref.shape[2]
    vsize = du_ref.shape[2]
    heads = du_ref.shape[0]
    t_ids, s_ids = coordinates(rows)
    strict = s_ids < t_ids

    @pl.when(pl.program_id(0) == 0)
    def _():
        gb_ref[...] = jnp.zeros_like(gb_ref)

    lanes = lax.broadcasted_iota(jnp.int32, gb_ref.shape, 1)
    grad_beta = jnp.zeros(gb_ref.shape, jnp.float32)
    for i in range(heads):
        head = base + pl.program_id(0) * heads + i
        key_float = k_ref[:, i * size : (i + 1) * size].astype(jnp.float32)
        value = v_ref[:, i * vsize : (i + 1) * vsize].astype(jnp.float32)
        gate = column(cc_ref[...], head)
        beta = column(beta_ref[...], head)
        gate_row = cr_ref[pl.ds(head, 1), :]
        key_scale = inverse_norm(key_float)
        key_normed = key_float * key_scale
        keys = cut(key_normed)
        pseudo = cut(u_ref[i])
        state = cut(ds_ref[i])
        trailing = jnp.exp(gate[rows - 1 :, :] - gate)
        grad_pseudo = du_ref[i] + trailing * dot3(keys, state)
        grad_key = dk_ref[i] + trailing * dot3(pseudo, state, NT)
        solved = dot3(cut(t_ref[i].T), cut(grad_pseudo))
        solved_parts = cut(solved)
        decay = decay_of(gate, gate_row, strict)
        grad_system = -dot3(solved_parts, pseudo, NT) * decay
        inner = dot3(keys, keys, NT)
        part = jnp.sum(solved * value, axis=-1, keepdims=True) + jnp.sum(
            grad_system * inner, axis=-1, keepdims=True
        )
        grad_beta = grad_beta + jnp.where(lanes == head, part, 0.0)
        grad_inner = beta * grad_system
        grad_key = grad_key + dot3(cut(grad_inner + grad_inner.T), keys)
        along = jnp.sum(grad_key * key_normed, axis=-1, keepdims=True)
        grad_key = key_scale * (grad_key - key_normed * along)
        gk_ref[:, i * size : (i + 1) * size] = grad_key.astype(gk_ref.dtype)
        gv_ref[:, i * vsize : (i + 1) * vsize] = (beta * solved).astype(gv_ref.dtype)
    gb_ref[...] += grad_beta


def local(query, key, value, beta, log_gate, level_weight, norm_gain, grad_out, grad_final_state):
    rows, heads, levels = level_weight.shape
    size = query.shape[1] // heads
    vsize = value.shape[1] // heads
    chunks = CHUNKS if heads % (CHUNKS * HEADS_STEP) == 0 else 1
    per = heads // chunks
    step = HEADS_STEP if per % HEADS_STEP == 0 else 1
    steps = per // step
    device = lax.axis_index("ctx")
    blocks = lax.axis_size("ctx")

    lower = jnp.tril(jnp.ones((rows, rows), jnp.float32))
    gates = lax.dot_general(lower, log_gate, NN, precision=topmost_level)
    gates_row = gates.T
    totals = lax.all_gather(gates[-1], "ctx")
    ids = jnp.arange(blocks)
    degrees = levels - 1

    def group_sum(match):
        return jnp.sum(jnp.where(match[:, None], totals, 0.0), axis=0)

    offset = jnp.zeros((heads,), jnp.float32)
    uppers, offsets, own_sums, partner_sums = [], [], [], []
    for degree in range(degrees):
        own = ids >> degree == device >> degree
        other = ids >> degree == (device >> degree) ^ 1
        is_upper = device >> degree & 1 == 1
        uppers.append(is_upper)
        offsets.append(offset)
        own_sums.append(group_sum(own))
        partner_sums.append(group_sum(other))
        offset = jnp.where(is_upper, offset + partner_sums[-1], offset)
    factors = [jnp.ones((rows, heads), jnp.float32)]
    for degree in range(degrees):
        reach = jnp.where(uppers[degree], jnp.exp(offsets[degree]), 0.0)
        factors.append(jnp.exp(gates) * reach[None, :])
    factor = jnp.stack(factors, axis=2)
    weight = (level_weight * factor).reshape(rows, heads * levels)
    factor = factor.reshape(rows, heads * levels)

    def whole(array):
        return pl.BlockSpec(array.shape, lambda g: (0,) * array.ndim)

    def wide(chunk, width):
        return pl.BlockSpec((rows, step * width), lambda g: (0, chunk * steps + g))

    def tall(*dims):
        return pl.BlockSpec((step,) + dims, lambda g: (g, 0, 0))

    def fixed(*dims):
        return pl.BlockSpec(dims, lambda g: (0,) * len(dims))

    def floats(*dims):
        return jax.ShapeDtypeStruct(dims, jnp.float32)

    def call(kernel, name, in_specs, outs, out_specs, dots):
        return pl.pallas_call(
            kernel,
            name=name,
            grid=(steps,),
            in_specs=in_specs,
            out_specs=out_specs,
            out_shape=outs,
            compiler_params=pltpu.CompilerParams(vmem_limit_bytes=VMEM_LIMIT),
            cost_estimate=pl.CostEstimate(
                flops=per * dots * 6 * rows * rows * size * 4,
                bytes_accessed=per * rows * size * 4 * 8,
                transcendentals=per * rows * rows,
            ),
        )

    prepared = []
    for chunk in range(chunks):
        prepared.append(
            call(
                functools.partial(prepare_kernel, chunk * per),
                f"prepare{chunk}",
                [wide(chunk, size), wide(chunk, vsize), whole(beta), whole(gates), whole(gates_row)],
                (floats(per, rows, rows), floats(per, rows, vsize), floats(per, size, vsize)),
                (tall(rows, rows), tall(rows, vsize), tall(size, vsize)),
                16,
            )(key, value, beta, gates, gates_row)
        )

    def part_of(vector, chunk):
        return vector[chunk * per : (chunk + 1) * per][:, None, None]

    aggregates = [state for _, _, state in prepared]
    partners = [[None] * degrees for _ in range(chunks)]
    for degree in range(degrees):
        for chunk in range(chunks):
            partner = from_partner(aggregates[chunk], "ctx", degree)
            partners[chunk][degree] = partner
            upper = uppers[degree]
            own_factor = jnp.where(upper, 1.0, jnp.exp(partner_sums[degree]))
            other_factor = jnp.where(upper, jnp.exp(own_sums[degree]), 1.0)
            aggregates[chunk] = (
                part_of(own_factor, chunk) * aggregates[chunk]
                + part_of(other_factor, chunk) * partner
            )

    rows_dev = grad_final_state.shape[0]
    full_rows = jnp.concatenate(aggregates).reshape(heads * size, vsize)
    own_rows = lax.dynamic_slice_in_dim(full_rows, device * rows_dev, rows_dev, 0)
    seeds = lax.dynamic_update_slice_in_dim(
        jnp.zeros((heads * size, vsize), jnp.float32), grad_final_state, device * rows_dev, 0
    ).reshape(heads, size, vsize)

    gain = norm_gain[None, :]
    finished = []
    for chunk in range(chunks):
        _, pseudo, _ = prepared[chunk]
        finished.append(
            call(
                functools.partial(finish_kernel, chunk * per, levels),
                f"finish{chunk}",
                [wide(chunk, size), wide(chunk, size), wide(chunk, vsize), tall(rows, vsize)]
                + [whole(gates), whole(gates_row), whole(weight), whole(factor), whole(gain)]
                + [tall(size, vsize)] * degrees,
                (
                    jax.ShapeDtypeStruct((rows, per * size), jnp.bfloat16),
                    floats(per, rows, size),
                    floats(per, rows, vsize),
                    floats(rows, heads * levels),
                    floats(1, vsize),
                )
                + (floats(per, size, vsize),) * degrees,
                (
                    wide(0, size),
                    tall(rows, size),
                    tall(rows, vsize),
                    fixed(rows, heads * levels),
                    fixed(1, vsize),
                )
                + (tall(size, vsize),) * degrees,
                6 + 3 * degrees,
            )(
                query, key, grad_out, pseudo, gates, gates_row, weight, factor, gain,
                *partners[chunk],
            )
        )
    grad_gain = lax.psum(sum(result[4] for result in finished)[0], "ctx")

    adjoints = [seeds[chunk * per : (chunk + 1) * per] for chunk in range(chunks)]
    for degree in reversed(range(degrees)):
        for chunk in range(chunks):
            adjoint = adjoints[chunk]
            upper = uppers[degree]
            send_factor = jnp.where(upper, jnp.exp(own_sums[degree]), 1.0)
            keep_factor = jnp.where(upper, 1.0, jnp.exp(partner_sums[degree]))
            outgoing = finished[chunk][5 + degree] + part_of(send_factor, chunk) * adjoint
            incoming = from_partner(outgoing, "ctx", degree)
            adjoints[chunk] = part_of(keep_factor, chunk) * adjoint + incoming

    backs = []
    for chunk in range(chunks):
        inverse, pseudo, _ = prepared[chunk]
        grad_key, grad_pseudo = finished[chunk][1:3]
        backs.append(
            call(
                functools.partial(back_kernel, chunk * per),
                f"back{chunk}",
                [wide(chunk, size), wide(chunk, vsize), whole(beta), whole(gates), whole(gates_row)]
                + [tall(rows, rows), tall(rows, vsize), tall(rows, size), tall(rows, vsize)]
                + [tall(size, vsize)],
                (
                    jax.ShapeDtypeStruct((rows, per * size), jnp.bfloat16),
                    jax.ShapeDtypeStruct((rows, per * vsize), jnp.bfloat16),
                    floats(rows, heads),
                ),
                (wide(0, size), wide(0, vsize), fixed(rows, heads)),
                6,
            )(
                key, value, beta, gates, gates_row, inverse, pseudo, grad_key, grad_pseudo,
                adjoints[chunk],
            )
        )
    return (
        jnp.concatenate([result[0] for result in finished], axis=1),
        jnp.concatenate([result[0] for result in backs], axis=1),
        jnp.concatenate([result[1] for result in backs], axis=1),
        sum(result[2] for result in backs),
        sum(result[3] for result in finished).reshape(rows, heads, levels),
        grad_gain,
        own_rows,
    )


def solution(mesh):
    in_specs = (
        P(("rep", "ctx"), None),
        P(("rep", "ctx"), None),
        P(("rep", "ctx"), None),
        P(("rep", "ctx"), None),
        P(("rep", "ctx"), None),
        P(("rep", "ctx"), None, None),
        P(),
        P(("rep", "ctx"), None),
        P(("rep", "ctx"), None),
    )
    out_specs = (
        P(("rep", "ctx"), None),
        P(("rep", "ctx"), None),
        P(("rep", "ctx"), None),
        P(("rep", "ctx"), None),
        P(("rep", "ctx"), None, None),
        P("rep"),
        P(("rep", "ctx"), None),
    )
    return jax.shard_map(local, mesh=mesh, in_specs=in_specs, out_specs=out_specs, check_vma=False)
```

```python
import functools

import jax
import jax.numpy as jnp
from jax import lax
from jax.experimental import pallas as pl
from jax.experimental.pallas import tpu as pltpu
from jax.sharding import PartitionSpec as P

epsilon = 1e-06
topmost_level = lax.Precision.HIGHEST
NN = (((1,), (0,)), ((), ()))
NT = (((1,), (1,)), ((), ()))
CHUNKS = 4
HEADS_STEP = 2
VMEM_LIMIT = 48 * 2**20


def from_partner(value, axis, bit):
    mask = 2**bit
    pairs = [(source, source ^ mask) for source in range(lax.axis_size(axis))]
    return lax.ppermute(value, axis, pairs)


def cut(x):
    high = x.astype(jnp.bfloat16)
    return high, (x - high.astype(jnp.float32)).astype(jnp.bfloat16)


def dot1(a, b, dims=NN):
    return lax.dot_general(a, b, dims, preferred_element_type=jnp.float32)


def dot3(a, b, dims=NN):
    left = jnp.concatenate([a[0], a[1], a[0]], axis=1)
    right = jnp.concatenate([b[0], b[0], b[1]], axis=0 if dims is NN else 1)
    return dot1(left, right, dims)


def dot2_right(a, b, dims=NN):
    left = jnp.concatenate([a[0], a[1]], axis=1)
    right = jnp.concatenate([b, b], axis=0 if dims is NN else 1)
    return dot1(left, right, dims)


def dot2_left(a, b, dims=NN):
    left = jnp.concatenate([a, a], axis=1)
    right = jnp.concatenate([b[0], b[1]], axis=0 if dims is NN else 1)
    return dot1(left, right, dims)


def column(values, lane):
    lanes = lax.broadcasted_iota(jnp.int32, values.shape, 1)
    return jnp.sum(jnp.where(lanes == lane, values, 0.0), axis=1, keepdims=True)


def inverse_norm(values):
    return lax.rsqrt(jnp.sum(values * values, axis=-1, keepdims=True) + epsilon)


def coordinates(rows):
    shape = (rows, rows)
    return lax.broadcasted_iota(jnp.int32, shape, 0), lax.broadcasted_iota(jnp.int32, shape, 1)


def decay_of(gate_column, gate_row, keep):
    return jnp.exp(jnp.where(keep, gate_column - gate_row, -jnp.inf))


def prepare_kernel(base, k_ref, v_ref, beta_ref, cc_ref, cr_ref, t_ref, u_ref, s_ref):
    rows = k_ref.shape[0]
    width = t_ref.shape[2]
    size = s_ref.shape[1]
    t_ids, s_ids = coordinates(rows)
    systems = []
    for i in range(t_ref.shape[0]):
        head = base + pl.program_id(0) * t_ref.shape[0] + i
        key = k_ref[:, i * size : (i + 1) * size]
        gate = column(cc_ref[...], head)
        beta = column(beta_ref[...], head)
        gate_row = cr_ref[pl.ds(head, 1), :]
        key_float = key.astype(jnp.float32)
        key_normed = key_float * inverse_norm(key_float)
        keys = cut(key_normed)
        inner = dot3(keys, keys, NT)
        systems.append(
            beta * decay_of(gate, gate_row, s_ids < t_ids) * inner
        )
        systems[-1] = (systems[-1], gate, beta, key_normed)
    inverses = []
    for system, _, _, _ in systems:
        first = jnp.where((t_ids ^ s_ids) == 1, system, 0.0)
        inverses.append(jnp.where(t_ids == s_ids, 1.0, 0.0) - first)
    span = 2
    while span < rows:
        gap = t_ids ^ s_ids
        keep = (gap >= span) & (gap < 2 * span)
        for i, (system, _, _, _) in enumerate(systems):
            parts = cut(inverses[i])
            mixed = dot3(cut(jnp.where(keep, system, 0.0)), parts)
            inverses[i] = inverses[i] - dot3(parts, cut(mixed))
        span *= 2
    for i, (_, gate, beta, key_normed) in enumerate(systems):
        value = v_ref[:, i * u_ref.shape[2] : (i + 1) * u_ref.shape[2]].astype(jnp.float32)
        pseudo = dot3(cut(inverses[i]), cut(beta * value))
        trailing = jnp.exp(gate[rows - 1 :, :] - gate)
        state = dot3(cut((key_normed * trailing).T), cut(pseudo))
        t_ref[i] = inverses[i]
        u_ref[i] = pseudo
        s_ref[i] = state


def finish_kernel(
    base, levels, q_ref, k_ref, go_ref, u_ref, cc_ref, cr_ref, w_ref, f_ref, gain_ref, *refs
):
    bucket_refs = refs[: levels - 1]
    gq_ref, dk_ref, du_ref, gl_ref, gg_ref = refs[levels - 1 : levels + 4]
    back_refs = refs[levels + 4 :]
    rows = q_ref.shape[0]
    size = dk_ref.shape[2]
    vsize = du_ref.shape[2]
    heads = du_ref.shape[0]
    t_ids, s_ids = coordinates(rows)

    @pl.when(pl.program_id(0) == 0)
    def _():
        gl_ref[...] = jnp.zeros_like(gl_ref)
        gg_ref[...] = jnp.zeros_like(gg_ref)

    level_lanes = lax.broadcasted_iota(jnp.int32, gl_ref.shape, 1)
    grad_level = jnp.zeros(gl_ref.shape, jnp.float32)
    grad_gain = jnp.zeros(gg_ref.shape, jnp.float32)
    for i in range(heads):
        head = base + pl.program_id(0) * heads + i
        query = q_ref[:, i * size : (i + 1) * size]
        key = k_ref[:, i * size : (i + 1) * size]
        grad_out = go_ref[:, i * vsize : (i + 1) * vsize].astype(jnp.float32)
        gate = column(cc_ref[...], head)
        gate_row = cr_ref[pl.ds(head, 1), :]
        query_float = query.astype(jnp.float32)
        key_float = key.astype(jnp.float32)
        query_scale = inverse_norm(query_float)
        query_normed = query_float * query_scale
        key_normed = key_float * inverse_norm(key_float)
        queries = cut(query_normed)
        keys = cut(key_normed)
        pseudo = cut(u_ref[i])
        decay = decay_of(gate, gate_row, s_ids <= t_ids)
        scores = dot3(queries, keys, NT) * decay
        intra = dot3(cut(scores), pseudo)
        weight0 = column(w_ref[...], head * levels)
        mixture = weight0 * intra
        weights, crosses, buckets = [], [], []
        for l in range(levels - 1):
            bucket = cut(bucket_refs[l][i])
            cross = dot3(queries, bucket)
            weight = column(w_ref[...], head * levels + 1 + l)
            mixture = mixture + weight * cross
            weights.append(weight)
            crosses.append(cross)
            buckets.append(bucket)
        scale = lax.rsqrt(jnp.mean(mixture * mixture, axis=-1, keepdims=True) + epsilon)
        unit = mixture * scale
        grad_gain = grad_gain + jnp.sum(grad_out * unit, axis=0, keepdims=True)
        grad_unit = grad_out * gain_ref[...]
        grad_mix = scale * (
            grad_unit - unit * jnp.mean(grad_unit * unit, axis=-1, keepdims=True)
        )
        part = jnp.sum(grad_mix * intra, axis=-1, keepdims=True)
        grad_level = grad_level + jnp.where(level_lanes == head * levels, part, 0.0)
        grad_intra = weight0 * grad_mix
        grad_intra_parts = cut(grad_intra)
        grad_scores = dot3(grad_intra_parts, pseudo, NT) * decay
        grad_query = dot3(cut(grad_scores), keys)
        dk_ref[i] = dot3(cut(grad_scores.T), queries)
        du_ref[i] = dot3(cut(scores.T), grad_intra_parts)
        query_turned = cut(query_normed.T)
        for l in range(levels - 1):
            lane = head * levels + 1 + l
            part = jnp.sum(grad_mix * crosses[l], axis=-1, keepdims=True)
            part = part * column(f_ref[...], lane)
            grad_level = grad_level + jnp.where(level_lanes == lane, part, 0.0)
            weighted = cut(weights[l] * grad_mix)
            grad_query = grad_query + dot3(weighted, buckets[l], NT)
            back_refs[l][i] = dot3(query_turned, weighted)
        along = jnp.sum(grad_query * query_normed, axis=-1, keepdims=True)
        grad_query = query_scale * (grad_query - query_normed * along)
        gq_ref[:, i * size : (i + 1) * size] = grad_query.astype(gq_ref.dtype)
    gl_ref[...] += grad_level
    gg_ref[...] += grad_gain


def back_kernel(
    base, k_ref, v_ref, beta_ref, cc_ref, cr_ref, t_ref, u_ref, dk_ref, du_ref, ds_ref,
    gk_ref, gv_ref, gb_ref,
):
    rows = k_ref.shape[0]
    size = dk_ref.shape[2]
    vsize = du_ref.shape[2]
    heads = du_ref.shape[0]
    t_ids, s_ids = coordinates(rows)
    strict = s_ids < t_ids

    @pl.when(pl.program_id(0) == 0)
    def _():
        gb_ref[...] = jnp.zeros_like(gb_ref)

    lanes = lax.broadcasted_iota(jnp.int32, gb_ref.shape, 1)
    grad_beta = jnp.zeros(gb_ref.shape, jnp.float32)
    for i in range(heads):
        head = base + pl.program_id(0) * heads + i
        key_float = k_ref[:, i * size : (i + 1) * size].astype(jnp.float32)
        value = v_ref[:, i * vsize : (i + 1) * vsize].astype(jnp.float32)
        gate = column(cc_ref[...], head)
        beta = column(beta_ref[...], head)
        gate_row = cr_ref[pl.ds(head, 1), :]
        key_scale = inverse_norm(key_float)
        key_normed = key_float * key_scale
        keys = cut(key_normed)
        pseudo = cut(u_ref[i])
        state = cut(ds_ref[i])
        trailing = jnp.exp(gate[rows - 1 :, :] - gate)
        grad_pseudo = du_ref[i] + trailing * dot3(keys, state)
        grad_key = dk_ref[i] + trailing * dot3(pseudo, state, NT)
        solved = dot3(cut(t_ref[i].T), cut(grad_pseudo))
        solved_parts = cut(solved)
        decay = decay_of(gate, gate_row, strict)
        grad_system = -dot3(solved_parts, pseudo, NT) * decay
        inner = dot3(keys, keys, NT)
        part = jnp.sum(solved * value, axis=-1, keepdims=True) + jnp.sum(
            grad_system * inner, axis=-1, keepdims=True
        )
        grad_beta = grad_beta + jnp.where(lanes == head, part, 0.0)
        grad_inner = beta * grad_system
        grad_key = grad_key + dot3(cut(grad_inner + grad_inner.T), keys)
        along = jnp.sum(grad_key * key_normed, axis=-1, keepdims=True)
        grad_key = key_scale * (grad_key - key_normed * along)
        gk_ref[:, i * size : (i + 1) * size] = grad_key.astype(gk_ref.dtype)
        gv_ref[:, i * vsize : (i + 1) * vsize] = (beta * solved).astype(gv_ref.dtype)
    gb_ref[...] += grad_beta


def local(query, key, value, beta, log_gate, level_weight, norm_gain, grad_out, grad_final_state):
    rows, heads, levels = level_weight.shape
    size = query.shape[1] // heads
    vsize = value.shape[1] // heads
    chunks = CHUNKS if heads % (CHUNKS * HEADS_STEP) == 0 else 1
    per = heads // chunks
    step = HEADS_STEP if per % HEADS_STEP == 0 else 1
    steps = per // step
    device = lax.axis_index("ctx")

    lower = jnp.tril(jnp.ones((rows, rows), jnp.float32))
    gates = lax.dot_general(lower, log_gate, NN, precision=topmost_level)
    gates_row = gates.T
    degrees = levels - 1
    top = degrees - 1
    half = 2**top
    unit = min(half, 2)
    hops = [[(half - unit + k, half + k) for k in range(unit)]]
    for stage in range(1, half // unit):
        hops.append(
            [(half + (stage - 1) * unit + k, half + stage * unit + k) for k in range(unit)]
        )

    offset = jnp.zeros((heads,), jnp.float32)
    group_total = gates[-1]
    uppers, offsets, own_sums, partner_sums = [], [], [], []
    for degree in range(degrees):
        is_upper = device >> degree & 1 == 1
        partner_total = from_partner(group_total, "ctx", degree)
        uppers.append(is_upper)
        offsets.append(offset)
        own_sums.append(group_total)
        partner_sums.append(partner_total)
        offset = jnp.where(is_upper, offset + partner_total, offset)
        group_total = group_total + partner_total
    factors = [jnp.ones((rows, heads), jnp.float32)]
    for degree in range(degrees):
        reach = jnp.where(uppers[degree], jnp.exp(offsets[degree]), 0.0)
        factors.append(jnp.exp(gates) * reach[None, :])
    factor = jnp.stack(factors, axis=2)
    weight = (level_weight * factor).reshape(rows, heads * levels)
    factor = factor.reshape(rows, heads * levels)

    def whole(array):
        return pl.BlockSpec(array.shape, lambda g: (0,) * array.ndim)

    def wide(chunk, width):
        return pl.BlockSpec((rows, step * width), lambda g: (0, chunk * steps + g))

    def tall(*dims):
        return pl.BlockSpec((step,) + dims, lambda g: (g, 0, 0))

    def fixed(*dims):
        return pl.BlockSpec(dims, lambda g: (0,) * len(dims))

    def floats(*dims):
        return jax.ShapeDtypeStruct(dims, jnp.float32)

    def call(kernel, name, in_specs, outs, out_specs, dots):
        return pl.pallas_call(
            kernel,
            name=name,
            grid=(steps,),
            in_specs=in_specs,
            out_specs=out_specs,
            out_shape=outs,
            compiler_params=pltpu.CompilerParams(vmem_limit_bytes=VMEM_LIMIT),
            cost_estimate=pl.CostEstimate(
                flops=per * dots * 6 * rows * rows * size * 4,
                bytes_accessed=per * rows * size * 4 * 8,
                transcendentals=per * rows * rows,
            ),
        )

    prepared = []
    for chunk in range(chunks):
        prepared.append(
            call(
                functools.partial(prepare_kernel, chunk * per),
                f"prepare{chunk}",
                [wide(chunk, size), wide(chunk, vsize), whole(beta), whole(gates), whole(gates_row)],
                (floats(per, rows, rows), floats(per, rows, vsize), floats(per, size, vsize)),
                (tall(rows, rows), tall(rows, vsize), tall(size, vsize)),
                16,
            )(key, value, beta, gates, gates_row)
        )

    def part_of(vector, chunk):
        return vector[chunk * per : (chunk + 1) * per][:, None, None]

    aggregates = [state for _, _, state in prepared]
    partners = [[None] * degrees for _ in range(chunks)]
    for degree in range(top):
        upper = uppers[degree]
        own_factor = jnp.where(upper, 1.0, jnp.exp(partner_sums[degree]))
        other_factor = jnp.where(upper, jnp.exp(own_sums[degree]), 1.0)
        for chunk in range(chunks):
            partner = from_partner(aggregates[chunk], "ctx", degree)
            partners[chunk][degree] = partner
            aggregates[chunk] = (
                part_of(own_factor, chunk) * aggregates[chunk]
                + part_of(other_factor, chunk) * partner
            )
    for chunk in range(chunks):
        passed = lax.ppermute(aggregates[chunk], "ctx", hops[0])
        gathered = passed
        for pairs in hops[1:]:
            passed = lax.ppermute(passed, "ctx", pairs)
            gathered = gathered + passed
        partners[chunk][top] = gathered

    rows_dev = grad_final_state.shape[0]
    own_start = device * rows_dev
    partner_start = (device ^ half) * rows_dev
    own_factor = jnp.where(uppers[top], 1.0, jnp.exp(partner_sums[top]))
    other_factor = jnp.where(uppers[top], jnp.exp(own_sums[top]), 1.0)

    def factor_rows(vector):
        spread = jnp.broadcast_to(vector[:, None], (heads, size)).reshape(heads * size, 1)
        return lax.dynamic_slice_in_dim(spread, own_start, rows_dev, 0)

    full_rows = jnp.concatenate(aggregates).reshape(heads * size, vsize)
    sent_rows = lax.dynamic_slice_in_dim(full_rows, partner_start, rows_dev, 0)
    own_rows = factor_rows(own_factor) * lax.dynamic_slice_in_dim(
        full_rows, own_start, rows_dev, 0
    ) + factor_rows(other_factor) * from_partner(sent_rows, "ctx", top)
    partner_seed = from_partner(grad_final_state, "ctx", top)
    seeds = jnp.zeros((heads * size, vsize), jnp.float32)
    seeds = lax.dynamic_update_slice_in_dim(seeds, grad_final_state, own_start, 0)
    seeds = lax.dynamic_update_slice_in_dim(seeds, partner_seed, partner_start, 0)
    seeds = own_factor[:, None, None] * seeds.reshape(heads, size, vsize)

    gain = norm_gain[None, :]
    finished = []
    for chunk in range(chunks):
        _, pseudo, _ = prepared[chunk]
        finished.append(
            call(
                functools.partial(finish_kernel, chunk * per, levels),
                f"finish{chunk}",
                [wide(chunk, size), wide(chunk, size), wide(chunk, vsize), tall(rows, vsize)]
                + [whole(gates), whole(gates_row), whole(weight), whole(factor), whole(gain)]
                + [tall(size, vsize)] * degrees,
                (
                    jax.ShapeDtypeStruct((rows, per * size), jnp.bfloat16),
                    floats(per, rows, size),
                    floats(per, rows, vsize),
                    floats(rows, heads * levels),
                    floats(1, vsize),
                )
                + (floats(per, size, vsize),) * degrees,
                (
                    wide(0, size),
                    tall(rows, size),
                    tall(rows, vsize),
                    fixed(rows, heads * levels),
                    fixed(1, vsize),
                )
                + (tall(size, vsize),) * degrees,
                6 + 3 * degrees,
            )(
                query, key, grad_out, pseudo, gates, gates_row, weight, factor, gain,
                *partners[chunk],
            )
        )
    grad_gain = sum(result[4] for result in finished)[0]
    for degree in range(degrees):
        grad_gain = grad_gain + from_partner(grad_gain, "ctx", degree)

    adjoints = []
    for chunk in range(chunks):
        carried = finished[chunk][5 + top]
        for pairs in reversed(hops[1:]):
            back_pairs = [(target, source) for source, target in pairs]
            carried = carried + lax.ppermute(carried, "ctx", back_pairs)
        back_pairs = [(target, source) for source, target in hops[0]]
        carried = lax.ppermute(carried, "ctx", back_pairs)
        adjoints.append(seeds[chunk * per : (chunk + 1) * per] + carried)
    for degree in reversed(range(top)):
        upper = uppers[degree]
        send_factor = jnp.where(upper, jnp.exp(own_sums[degree]), 1.0)
        keep_factor = jnp.where(upper, 1.0, jnp.exp(partner_sums[degree]))
        for chunk in range(chunks):
            adjoint = adjoints[chunk]
            outgoing = finished[chunk][5 + degree] + part_of(send_factor, chunk) * adjoint
            incoming = from_partner(outgoing, "ctx", degree)
            adjoints[chunk] = part_of(keep_factor, chunk) * adjoint + incoming

    backs = []
    for chunk in range(chunks):
        inverse, pseudo, _ = prepared[chunk]
        grad_key, grad_pseudo = finished[chunk][1:3]
        backs.append(
            call(
                functools.partial(back_kernel, chunk * per),
                f"back{chunk}",
                [wide(chunk, size), wide(chunk, vsize), whole(beta), whole(gates), whole(gates_row)]
                + [tall(rows, rows), tall(rows, vsize), tall(rows, size), tall(rows, vsize)]
                + [tall(size, vsize)],
                (
                    jax.ShapeDtypeStruct((rows, per * size), jnp.bfloat16),
                    jax.ShapeDtypeStruct((rows, per * vsize), jnp.bfloat16),
                    floats(rows, heads),
                ),
                (wide(0, size), wide(0, vsize), fixed(rows, heads)),
                6,
            )(
                key, value, beta, gates, gates_row, inverse, pseudo, grad_key, grad_pseudo,
                adjoints[chunk],
            )
        )
    return (
        jnp.concatenate([result[0] for result in finished], axis=1),
        jnp.concatenate([result[0] for result in backs], axis=1),
        jnp.concatenate([result[1] for result in backs], axis=1),
        sum(result[2] for result in backs),
        sum(result[3] for result in finished).reshape(rows, heads, levels),
        grad_gain,
        own_rows,
    )


def solution(mesh):
    in_specs = (
        P(("rep", "ctx"), None),
        P(("rep", "ctx"), None),
        P(("rep", "ctx"), None),
        P(("rep", "ctx"), None),
        P(("rep", "ctx"), None),
        P(("rep", "ctx"), None, None),
        P(),
        P(("rep", "ctx"), None),
        P(("rep", "ctx"), None),
    )
    out_specs = (
        P(("rep", "ctx"), None),
        P(("rep", "ctx"), None),
        P(("rep", "ctx"), None),
        P(("rep", "ctx"), None),
        P(("rep", "ctx"), None, None),
        P("rep"),
        P(("rep", "ctx"), None),
    )
    return jax.shard_map(local, mesh=mesh, in_specs=in_specs, out_specs=out_specs, check_vma=False)
```

```python
import functools

import jax
import jax.numpy as jnp
from jax import lax
from jax.experimental import pallas as pl
from jax.experimental.pallas import tpu as pltpu
from jax.sharding import PartitionSpec as P

epsilon = 1e-06
topmost_level = lax.Precision.HIGHEST
NN = (((1,), (0,)), ((), ()))
NT = (((1,), (1,)), ((), ()))
CHUNKS = 4
HEADS_STEP = 4
VMEM_LIMIT = 48 * 2**20


def from_partner(value, axis, bit):
    mask = 2**bit
    pairs = [(source, source ^ mask) for source in range(lax.axis_size(axis))]
    return lax.ppermute(value, axis, pairs)


def cut(x):
    high = x.astype(jnp.bfloat16)
    return high, (x - high.astype(jnp.float32)).astype(jnp.bfloat16)


def dot1(a, b, dims=NN):
    return lax.dot_general(a, b, dims, preferred_element_type=jnp.float32)


def dot3(a, b, dims=NN):
    left = jnp.concatenate([a[0], a[1], a[0]], axis=1)
    right = jnp.concatenate([b[0], b[0], b[1]], axis=0 if dims is NN else 1)
    return dot1(left, right, dims)


def dot2_right(a, b, dims=NN):
    left = jnp.concatenate([a[0], a[1]], axis=1)
    right = jnp.concatenate([b, b], axis=0 if dims is NN else 1)
    return dot1(left, right, dims)


def dot2_left(a, b, dims=NN):
    left = jnp.concatenate([a, a], axis=1)
    right = jnp.concatenate([b[0], b[1]], axis=0 if dims is NN else 1)
    return dot1(left, right, dims)


def column(values, lane):
    lanes = lax.broadcasted_iota(jnp.int32, values.shape, 1)
    return jnp.sum(jnp.where(lanes == lane, values, 0.0), axis=1, keepdims=True)


def inverse_norm(values):
    return lax.rsqrt(jnp.sum(values * values, axis=-1, keepdims=True) + epsilon)


def coordinates(rows):
    shape = (rows, rows)
    return lax.broadcasted_iota(jnp.int32, shape, 0), lax.broadcasted_iota(jnp.int32, shape, 1)


def decay_of(gate_column, gate_row, keep):
    return jnp.exp(jnp.where(keep, gate_column - gate_row, -jnp.inf))


def prepare_kernel(base, k_ref, v_ref, beta_ref, cc_ref, cr_ref, t_ref, u_ref, s_ref):
    rows = k_ref.shape[0]
    width = t_ref.shape[2]
    size = s_ref.shape[1]
    t_ids, s_ids = coordinates(rows)
    systems = []
    for i in range(t_ref.shape[0]):
        head = base + pl.program_id(0) * t_ref.shape[0] + i
        key = k_ref[:, i * size : (i + 1) * size]
        gate = column(cc_ref[...], head)
        beta = column(beta_ref[...], head)
        gate_row = cr_ref[pl.ds(head, 1), :]
        key_float = key.astype(jnp.float32)
        key_normed = key_float * inverse_norm(key_float)
        keys = cut(key_normed)
        inner = dot3(keys, keys, NT)
        systems.append(
            beta * decay_of(gate, gate_row, s_ids < t_ids) * inner
        )
        systems[-1] = (systems[-1], gate, beta, key_normed)
    inverses = []
    for system, _, _, _ in systems:
        first = jnp.where((t_ids ^ s_ids) == 1, system, 0.0)
        inverses.append(jnp.where(t_ids == s_ids, 1.0, 0.0) - first)
    span = 2
    while span < rows:
        gap = t_ids ^ s_ids
        keep = (gap >= span) & (gap < 2 * span)
        for i, (system, _, _, _) in enumerate(systems):
            parts = cut(inverses[i])
            mixed = dot3(cut(jnp.where(keep, system, 0.0)), parts)
            inverses[i] = inverses[i] - dot3(parts, cut(mixed))
        span *= 2
    for i, (_, gate, beta, key_normed) in enumerate(systems):
        value = v_ref[:, i * u_ref.shape[2] : (i + 1) * u_ref.shape[2]].astype(jnp.float32)
        pseudo = dot3(cut(inverses[i]), cut(beta * value))
        trailing = jnp.exp(gate[rows - 1 :, :] - gate)
        state = dot3(cut((key_normed * trailing).T), cut(pseudo))
        t_ref[i] = inverses[i]
        u_ref[i] = pseudo
        s_ref[i] = state


def finish_kernel(
    base, levels, q_ref, k_ref, go_ref, u_ref, cc_ref, cr_ref, w_ref, f_ref, gain_ref, *refs
):
    bucket_refs = refs[: levels - 1]
    gq_ref, dk_ref, du_ref, gl_ref, gg_ref = refs[levels - 1 : levels + 4]
    back_refs = refs[levels + 4 :]
    rows = q_ref.shape[0]
    size = dk_ref.shape[2]
    vsize = du_ref.shape[2]
    heads = du_ref.shape[0]
    t_ids, s_ids = coordinates(rows)

    @pl.when(pl.program_id(0) == 0)
    def _():
        gl_ref[...] = jnp.zeros_like(gl_ref)
        gg_ref[...] = jnp.zeros_like(gg_ref)

    level_lanes = lax.broadcasted_iota(jnp.int32, gl_ref.shape, 1)
    grad_level = jnp.zeros(gl_ref.shape, jnp.float32)
    grad_gain = jnp.zeros(gg_ref.shape, jnp.float32)
    for i in range(heads):
        head = base + pl.program_id(0) * heads + i
        query = q_ref[:, i * size : (i + 1) * size]
        key = k_ref[:, i * size : (i + 1) * size]
        grad_out = go_ref[:, i * vsize : (i + 1) * vsize].astype(jnp.float32)
        gate = column(cc_ref[...], head)
        gate_row = cr_ref[pl.ds(head, 1), :]
        query_float = query.astype(jnp.float32)
        key_float = key.astype(jnp.float32)
        query_scale = inverse_norm(query_float)
        query_normed = query_float * query_scale
        key_normed = key_float * inverse_norm(key_float)
        queries = cut(query_normed)
        keys = cut(key_normed)
        pseudo = cut(u_ref[i])
        decay = decay_of(gate, gate_row, s_ids <= t_ids)
        scores = dot3(queries, keys, NT) * decay
        intra = dot3(cut(scores), pseudo)
        weight0 = column(w_ref[...], head * levels)
        mixture = weight0 * intra
        weights, crosses, buckets = [], [], []
        for l in range(levels - 1):
            bucket = cut(bucket_refs[l][i])
            cross = dot3(queries, bucket)
            weight = column(w_ref[...], head * levels + 1 + l)
            mixture = mixture + weight * cross
            weights.append(weight)
            crosses.append(cross)
            buckets.append(bucket)
        scale = lax.rsqrt(jnp.mean(mixture * mixture, axis=-1, keepdims=True) + epsilon)
        unit = mixture * scale
        grad_gain = grad_gain + jnp.sum(grad_out * unit, axis=0, keepdims=True)
        grad_unit = grad_out * gain_ref[...]
        grad_mix = scale * (
            grad_unit - unit * jnp.mean(grad_unit * unit, axis=-1, keepdims=True)
        )
        part = jnp.sum(grad_mix * intra, axis=-1, keepdims=True)
        grad_level = grad_level + jnp.where(level_lanes == head * levels, part, 0.0)
        grad_intra = weight0 * grad_mix
        grad_intra_parts = cut(grad_intra)
        grad_scores = dot3(grad_intra_parts, pseudo, NT) * decay
        grad_query = dot3(cut(grad_scores), keys)
        dk_ref[i] = dot3(cut(grad_scores.T), queries)
        du_ref[i] = dot3(cut(scores.T), grad_intra_parts)
        query_turned = cut(query_normed.T)
        for l in range(levels - 1):
            lane = head * levels + 1 + l
            part = jnp.sum(grad_mix * crosses[l], axis=-1, keepdims=True)
            part = part * column(f_ref[...], lane)
            grad_level = grad_level + jnp.where(level_lanes == lane, part, 0.0)
            weighted = cut(weights[l] * grad_mix)
            grad_query = grad_query + dot3(weighted, buckets[l], NT)
            back_refs[l][i] = dot3(query_turned, weighted)
        along = jnp.sum(grad_query * query_normed, axis=-1, keepdims=True)
        grad_query = query_scale * (grad_query - query_normed * along)
        gq_ref[:, i * size : (i + 1) * size] = grad_query.astype(gq_ref.dtype)
    gl_ref[...] += grad_level
    gg_ref[...] += grad_gain


def back_kernel(
    base, k_ref, v_ref, beta_ref, cc_ref, cr_ref, t_ref, u_ref, dk_ref, du_ref, ds_ref,
    gk_ref, gv_ref, gb_ref,
):
    rows = k_ref.shape[0]
    size = dk_ref.shape[2]
    vsize = du_ref.shape[2]
    heads = du_ref.shape[0]
    t_ids, s_ids = coordinates(rows)
    strict = s_ids < t_ids

    @pl.when(pl.program_id(0) == 0)
    def _():
        gb_ref[...] = jnp.zeros_like(gb_ref)

    lanes = lax.broadcasted_iota(jnp.int32, gb_ref.shape, 1)
    grad_beta = jnp.zeros(gb_ref.shape, jnp.float32)
    for i in range(heads):
        head = base + pl.program_id(0) * heads + i
        key_float = k_ref[:, i * size : (i + 1) * size].astype(jnp.float32)
        value = v_ref[:, i * vsize : (i + 1) * vsize].astype(jnp.float32)
        gate = column(cc_ref[...], head)
        beta = column(beta_ref[...], head)
        gate_row = cr_ref[pl.ds(head, 1), :]
        key_scale = inverse_norm(key_float)
        key_normed = key_float * key_scale
        keys = cut(key_normed)
        pseudo = cut(u_ref[i])
        state = cut(ds_ref[i])
        trailing = jnp.exp(gate[rows - 1 :, :] - gate)
        grad_pseudo = du_ref[i] + trailing * dot3(keys, state)
        grad_key = dk_ref[i] + trailing * dot3(pseudo, state, NT)
        solved = dot3(cut(t_ref[i].T), cut(grad_pseudo))
        solved_parts = cut(solved)
        decay = decay_of(gate, gate_row, strict)
        grad_system = -dot3(solved_parts, pseudo, NT) * decay
        inner = dot3(keys, keys, NT)
        part = jnp.sum(solved * value, axis=-1, keepdims=True) + jnp.sum(
            grad_system * inner, axis=-1, keepdims=True
        )
        grad_beta = grad_beta + jnp.where(lanes == head, part, 0.0)
        grad_inner = beta * grad_system
        grad_key = grad_key + dot3(cut(grad_inner + grad_inner.T), keys)
        along = jnp.sum(grad_key * key_normed, axis=-1, keepdims=True)
        grad_key = key_scale * (grad_key - key_normed * along)
        gk_ref[:, i * size : (i + 1) * size] = grad_key.astype(gk_ref.dtype)
        gv_ref[:, i * vsize : (i + 1) * vsize] = (beta * solved).astype(gv_ref.dtype)
    gb_ref[...] += grad_beta


def local(query, key, value, beta, log_gate, level_weight, norm_gain, grad_out, grad_final_state):
    rows, heads, levels = level_weight.shape
    size = query.shape[1] // heads
    vsize = value.shape[1] // heads
    chunks = CHUNKS if heads % (CHUNKS * HEADS_STEP) == 0 else 1
    per = heads // chunks
    step = HEADS_STEP if per % HEADS_STEP == 0 else 1
    steps = per // step
    device = lax.axis_index("ctx")

    lower = jnp.tril(jnp.ones((rows, rows), jnp.float32))
    gates = lax.dot_general(lower, log_gate, NN, precision=topmost_level)
    gates_row = gates.T
    degrees = levels - 1
    top = degrees - 1
    half = 2**top
    unit = min(half, 2)
    hops = [[(half - unit + k, half + k) for k in range(unit)]]
    for stage in range(1, half // unit):
        hops.append(
            [(half + (stage - 1) * unit + k, half + stage * unit + k) for k in range(unit)]
        )

    offset = jnp.zeros((heads,), jnp.float32)
    group_total = gates[-1]
    uppers, offsets, own_sums, partner_sums = [], [], [], []
    for degree in range(degrees):
        is_upper = device >> degree & 1 == 1
        partner_total = from_partner(group_total, "ctx", degree)
        uppers.append(is_upper)
        offsets.append(offset)
        own_sums.append(group_total)
        partner_sums.append(partner_total)
        offset = jnp.where(is_upper, offset + partner_total, offset)
        group_total = group_total + partner_total
    factors = [jnp.ones((rows, heads), jnp.float32)]
    for degree in range(degrees):
        reach = jnp.where(uppers[degree], jnp.exp(offsets[degree]), 0.0)
        factors.append(jnp.exp(gates) * reach[None, :])
    factor = jnp.stack(factors, axis=2)
    weight = (level_weight * factor).reshape(rows, heads * levels)
    factor = factor.reshape(rows, heads * levels)

    def whole(array):
        return pl.BlockSpec(array.shape, lambda g: (0,) * array.ndim)

    def wide(chunk, width):
        return pl.BlockSpec((rows, step * width), lambda g: (0, chunk * steps + g))

    def tall(*dims):
        return pl.BlockSpec((step,) + dims, lambda g: (g, 0, 0))

    def fixed(*dims):
        return pl.BlockSpec(dims, lambda g: (0,) * len(dims))

    def floats(*dims):
        return jax.ShapeDtypeStruct(dims, jnp.float32)

    def call(kernel, name, in_specs, outs, out_specs, dots):
        return pl.pallas_call(
            kernel,
            name=name,
            grid=(steps,),
            in_specs=in_specs,
            out_specs=out_specs,
            out_shape=outs,
            compiler_params=pltpu.CompilerParams(vmem_limit_bytes=VMEM_LIMIT),
            cost_estimate=pl.CostEstimate(
                flops=per * dots * 6 * rows * rows * size * 4,
                bytes_accessed=per * rows * size * 4 * 8,
                transcendentals=per * rows * rows,
            ),
        )

    prepared = []
    for chunk in range(chunks):
        prepared.append(
            call(
                functools.partial(prepare_kernel, chunk * per),
                f"prepare{chunk}",
                [wide(chunk, size), wide(chunk, vsize), whole(beta), whole(gates), whole(gates_row)],
                (floats(per, rows, rows), floats(per, rows, vsize), floats(per, size, vsize)),
                (tall(rows, rows), tall(rows, vsize), tall(size, vsize)),
                16,
            )(key, value, beta, gates, gates_row)
        )

    def part_of(vector, chunk):
        return vector[chunk * per : (chunk + 1) * per][:, None, None]

    aggregates = [state for _, _, state in prepared]
    partners = [[None] * degrees for _ in range(chunks)]
    for degree in range(top):
        upper = uppers[degree]
        own_factor = jnp.where(upper, 1.0, jnp.exp(partner_sums[degree]))
        other_factor = jnp.where(upper, jnp.exp(own_sums[degree]), 1.0)
        for chunk in range(chunks):
            partner = from_partner(aggregates[chunk], "ctx", degree)
            partners[chunk][degree] = partner
            aggregates[chunk] = (
                part_of(own_factor, chunk) * aggregates[chunk]
                + part_of(other_factor, chunk) * partner
            )
    for chunk in range(chunks):
        passed = lax.ppermute(aggregates[chunk], "ctx", hops[0])
        gathered = passed
        for pairs in hops[1:]:
            passed = lax.ppermute(passed, "ctx", pairs)
            gathered = gathered + passed
        partners[chunk][top] = gathered

    rows_dev = grad_final_state.shape[0]
    own_start = device * rows_dev
    partner_start = (device ^ half) * rows_dev
    own_factor = jnp.where(uppers[top], 1.0, jnp.exp(partner_sums[top]))
    other_factor = jnp.where(uppers[top], jnp.exp(own_sums[top]), 1.0)

    def factor_rows(vector):
        spread = jnp.broadcast_to(vector[:, None], (heads, size)).reshape(heads * size, 1)
        return lax.dynamic_slice_in_dim(spread, own_start, rows_dev, 0)

    full_rows = jnp.concatenate(aggregates).reshape(heads * size, vsize)
    sent_rows = lax.dynamic_slice_in_dim(full_rows, partner_start, rows_dev, 0)
    partner_seed = from_partner(grad_final_state, "ctx", top)
    seeds = jnp.zeros((heads * size, vsize), jnp.float32)
    seeds = lax.dynamic_update_slice_in_dim(seeds, grad_final_state, own_start, 0)
    seeds = lax.dynamic_update_slice_in_dim(seeds, partner_seed, partner_start, 0)
    seeds = own_factor[:, None, None] * seeds.reshape(heads, size, vsize)

    gain = norm_gain[None, :]
    finished = []
    for chunk in range(chunks):
        _, pseudo, _ = prepared[chunk]
        finished.append(
            call(
                functools.partial(finish_kernel, chunk * per, levels),
                f"finish{chunk}",
                [wide(chunk, size), wide(chunk, size), wide(chunk, vsize), tall(rows, vsize)]
                + [whole(gates), whole(gates_row), whole(weight), whole(factor), whole(gain)]
                + [tall(size, vsize)] * degrees,
                (
                    jax.ShapeDtypeStruct((rows, per * size), jnp.bfloat16),
                    floats(per, rows, size),
                    floats(per, rows, vsize),
                    floats(rows, heads * levels),
                    floats(1, vsize),
                )
                + (floats(per, size, vsize),) * degrees,
                (
                    wide(0, size),
                    tall(rows, size),
                    tall(rows, vsize),
                    fixed(rows, heads * levels),
                    fixed(1, vsize),
                )
                + (tall(size, vsize),) * degrees,
                6 + 3 * degrees,
            )(
                query, key, grad_out, pseudo, gates, gates_row, weight, factor, gain,
                *partners[chunk],
            )
        )
    def with_gain(array, gain_row):
        padded = jnp.pad(gain_row, ((0, 7), (0, 0)))
        return jnp.concatenate([array.reshape(-1, vsize), padded])

    grad_gain = sum(result[4] for result in finished)
    exchanged = from_partner(with_gain(sent_rows, grad_gain), "ctx", top)
    grad_gain = grad_gain + exchanged[rows_dev : rows_dev + 1]
    own_rows = (
        factor_rows(own_factor) * lax.dynamic_slice_in_dim(full_rows, own_start, rows_dev, 0)
        + factor_rows(other_factor) * exchanged[:rows_dev]
    )

    adjoints = []
    for chunk in range(chunks):
        carried = finished[chunk][5 + top]
        for pairs in reversed(hops[1:]):
            back_pairs = [(target, source) for source, target in pairs]
            carried = carried + lax.ppermute(carried, "ctx", back_pairs)
        back_pairs = [(target, source) for source, target in hops[0]]
        carried = lax.ppermute(carried, "ctx", back_pairs)
        adjoints.append(seeds[chunk * per : (chunk + 1) * per] + carried)
    for degree in reversed(range(top)):
        upper = uppers[degree]
        send_factor = jnp.where(upper, jnp.exp(own_sums[degree]), 1.0)
        keep_factor = jnp.where(upper, 1.0, jnp.exp(partner_sums[degree]))
        for chunk in range(chunks):
            adjoint = adjoints[chunk]
            outgoing = finished[chunk][5 + degree] + part_of(send_factor, chunk) * adjoint
            if chunk == chunks - 1:
                exchanged = from_partner(with_gain(outgoing, grad_gain), "ctx", degree)
                incoming = exchanged[: per * size].reshape(per, size, vsize)
                grad_gain = grad_gain + exchanged[per * size : per * size + 1]
            else:
                incoming = from_partner(outgoing, "ctx", degree)
            adjoints[chunk] = part_of(keep_factor, chunk) * adjoint + incoming

    backs = []
    for chunk in range(chunks):
        inverse, pseudo, _ = prepared[chunk]
        grad_key, grad_pseudo = finished[chunk][1:3]
        backs.append(
            call(
                functools.partial(back_kernel, chunk * per),
                f"back{chunk}",
                [wide(chunk, size), wide(chunk, vsize), whole(beta), whole(gates), whole(gates_row)]
                + [tall(rows, rows), tall(rows, vsize), tall(rows, size), tall(rows, vsize)]
                + [tall(size, vsize)],
                (
                    jax.ShapeDtypeStruct((rows, per * size), jnp.bfloat16),
                    jax.ShapeDtypeStruct((rows, per * vsize), jnp.bfloat16),
                    floats(rows, heads),
                ),
                (wide(0, size), wide(0, vsize), fixed(rows, heads)),
                6,
            )(
                key, value, beta, gates, gates_row, inverse, pseudo, grad_key, grad_pseudo,
                adjoints[chunk],
            )
        )
    return (
        jnp.concatenate([result[0] for result in finished], axis=1),
        jnp.concatenate([result[0] for result in backs], axis=1),
        jnp.concatenate([result[1] for result in backs], axis=1),
        sum(result[2] for result in backs),
        sum(result[3] for result in finished).reshape(rows, heads, levels),
        grad_gain[0],
        own_rows,
    )


def solution(mesh):
    in_specs = (
        P(("rep", "ctx"), None),
        P(("rep", "ctx"), None),
        P(("rep", "ctx"), None),
        P(("rep", "ctx"), None),
        P(("rep", "ctx"), None),
        P(("rep", "ctx"), None, None),
        P(),
        P(("rep", "ctx"), None),
        P(("rep", "ctx"), None),
    )
    out_specs = (
        P(("rep", "ctx"), None),
        P(("rep", "ctx"), None),
        P(("rep", "ctx"), None),
        P(("rep", "ctx"), None),
        P(("rep", "ctx"), None, None),
        P("rep"),
        P(("rep", "ctx"), None),
    )
    return jax.shard_map(local, mesh=mesh, in_specs=in_specs, out_specs=out_specs, check_vma=False)
```

```python
import functools

import jax
import jax.numpy as jnp
from jax import lax
from jax.experimental import pallas as pl
from jax.experimental.pallas import tpu as pltpu
from jax.sharding import PartitionSpec as P

epsilon = 1e-06
topmost_level = lax.Precision.HIGHEST
NN = (((1,), (0,)), ((), ()))
NT = (((1,), (1,)), ((), ()))
CHUNKS = 4
HEADS_STEP = 4
VMEM_LIMIT = 48 * 2**20


def from_partner(value, axis, bit):
    mask = 2**bit
    pairs = [(source, source ^ mask) for source in range(lax.axis_size(axis))]
    return lax.ppermute(value, axis, pairs)


def cut(x):
    high = x.astype(jnp.bfloat16)
    return high, (x - high.astype(jnp.float32)).astype(jnp.bfloat16)


def dot1(a, b, dims=NN):
    return lax.dot_general(a, b, dims, preferred_element_type=jnp.float32)


def dot3(a, b, dims=NN):
    left = jnp.concatenate([a[0], a[1], a[0]], axis=1)
    right = jnp.concatenate([b[0], b[0], b[1]], axis=0 if dims is NN else 1)
    return dot1(left, right, dims)


def dot2_right(a, b, dims=NN):
    left = jnp.concatenate([a[0], a[1]], axis=1)
    right = jnp.concatenate([b, b], axis=0 if dims is NN else 1)
    return dot1(left, right, dims)


def dot2_left(a, b, dims=NN):
    left = jnp.concatenate([a, a], axis=1)
    right = jnp.concatenate([b[0], b[1]], axis=0 if dims is NN else 1)
    return dot1(left, right, dims)


def column(values, lane):
    lanes = lax.broadcasted_iota(jnp.int32, values.shape, 1)
    return jnp.sum(jnp.where(lanes == lane, values, 0.0), axis=1, keepdims=True)


def inverse_norm(values):
    return lax.rsqrt(jnp.sum(values * values, axis=-1, keepdims=True) + epsilon)


def coordinates(rows):
    shape = (rows, rows)
    return lax.broadcasted_iota(jnp.int32, shape, 0), lax.broadcasted_iota(jnp.int32, shape, 1)


def decay_of(gate_column, gate_row, keep):
    return jnp.exp(jnp.where(keep, gate_column - gate_row, -jnp.inf))


def prepare_kernel(base, k_ref, v_ref, beta_ref, cc_ref, cr_ref, t_ref, u_ref, s_ref):
    rows = k_ref.shape[0]
    width = t_ref.shape[2]
    size = s_ref.shape[1]
    t_ids, s_ids = coordinates(rows)
    systems = []
    for i in range(t_ref.shape[0]):
        head = base + pl.program_id(0) * t_ref.shape[0] + i
        key = k_ref[:, i * size : (i + 1) * size]
        gate = column(cc_ref[...], head)
        beta = column(beta_ref[...], head)
        gate_row = cr_ref[pl.ds(head, 1), :]
        key_float = key.astype(jnp.float32)
        key_normed = key_float * inverse_norm(key_float)
        keys = cut(key_normed)
        inner = dot3(keys, keys, NT)
        systems.append(
            beta * decay_of(gate, gate_row, s_ids < t_ids) * inner
        )
        systems[-1] = (systems[-1], gate, beta, key_normed)
    inverses = []
    for system, _, _, _ in systems:
        first = jnp.where((t_ids ^ s_ids) == 1, system, 0.0)
        inverses.append(jnp.where(t_ids == s_ids, 1.0, 0.0) - first)
    span = 2
    while span < rows:
        gap = t_ids ^ s_ids
        keep = (gap >= span) & (gap < 2 * span)
        for i, (system, _, _, _) in enumerate(systems):
            parts = cut(inverses[i])
            mixed = dot3(cut(jnp.where(keep, system, 0.0)), parts)
            inverses[i] = inverses[i] - dot3(parts, cut(mixed))
        span *= 2
    for i, (_, gate, beta, key_normed) in enumerate(systems):
        value = v_ref[:, i * u_ref.shape[2] : (i + 1) * u_ref.shape[2]].astype(jnp.float32)
        pseudo = dot3(cut(inverses[i]), cut(beta * value))
        trailing = jnp.exp(gate[rows - 1 :, :] - gate)
        state = dot3(cut((key_normed * trailing).T), cut(pseudo))
        t_ref[i] = inverses[i]
        u_ref[i] = pseudo
        s_ref[i] = state


def finish_kernel(
    base, levels, q_ref, k_ref, go_ref, u_ref, cc_ref, cr_ref, w_ref, f_ref, gain_ref, *refs
):
    bucket_refs = refs[: levels - 1]
    gq_ref, dk_ref, du_ref, gl_ref, gg_ref = refs[levels - 1 : levels + 4]
    back_refs = refs[levels + 4 :]
    rows = q_ref.shape[0]
    size = dk_ref.shape[2]
    vsize = du_ref.shape[2]
    heads = du_ref.shape[0]
    t_ids, s_ids = coordinates(rows)

    @pl.when(pl.program_id(0) == 0)
    def _():
        gl_ref[...] = jnp.zeros_like(gl_ref)
        gg_ref[...] = jnp.zeros_like(gg_ref)

    level_lanes = lax.broadcasted_iota(jnp.int32, gl_ref.shape, 1)
    grad_level = jnp.zeros(gl_ref.shape, jnp.float32)
    grad_gain = jnp.zeros(gg_ref.shape, jnp.float32)
    for i in range(heads):
        head = base + pl.program_id(0) * heads + i
        query = q_ref[:, i * size : (i + 1) * size]
        key = k_ref[:, i * size : (i + 1) * size]
        grad_out = go_ref[:, i * vsize : (i + 1) * vsize].astype(jnp.float32)
        gate = column(cc_ref[...], head)
        gate_row = cr_ref[pl.ds(head, 1), :]
        query_float = query.astype(jnp.float32)
        key_float = key.astype(jnp.float32)
        query_scale = inverse_norm(query_float)
        query_normed = query_float * query_scale
        key_normed = key_float * inverse_norm(key_float)
        queries = cut(query_normed)
        keys = cut(key_normed)
        pseudo = cut(u_ref[i])
        decay = decay_of(gate, gate_row, s_ids <= t_ids)
        scores = dot3(queries, keys, NT) * decay
        intra = dot3(cut(scores), pseudo)
        weight0 = column(w_ref[...], head * levels)
        mixture = weight0 * intra
        weights, crosses, buckets = [], [], []
        for l in range(levels - 1):
            bucket = cut(bucket_refs[l][i])
            cross = dot3(queries, bucket)
            weight = column(w_ref[...], head * levels + 1 + l)
            mixture = mixture + weight * cross
            weights.append(weight)
            crosses.append(cross)
            buckets.append(bucket)
        scale = lax.rsqrt(jnp.mean(mixture * mixture, axis=-1, keepdims=True) + epsilon)
        unit = mixture * scale
        grad_gain = grad_gain + jnp.sum(grad_out * unit, axis=0, keepdims=True)
        grad_unit = grad_out * gain_ref[...]
        grad_mix = scale * (
            grad_unit - unit * jnp.mean(grad_unit * unit, axis=-1, keepdims=True)
        )
        part = jnp.sum(grad_mix * intra, axis=-1, keepdims=True)
        grad_level = grad_level + jnp.where(level_lanes == head * levels, part, 0.0)
        grad_intra = weight0 * grad_mix
        grad_intra_parts = cut(grad_intra)
        grad_scores = dot3(grad_intra_parts, pseudo, NT) * decay
        grad_query = dot3(cut(grad_scores), keys)
        dk_ref[i] = dot3(cut(grad_scores.T), queries)
        du_ref[i] = dot3(cut(scores.T), grad_intra_parts)
        query_turned = cut(query_normed.T)
        for l in range(levels - 1):
            lane = head * levels + 1 + l
            part = jnp.sum(grad_mix * crosses[l], axis=-1, keepdims=True)
            part = part * column(f_ref[...], lane)
            grad_level = grad_level + jnp.where(level_lanes == lane, part, 0.0)
            weighted = cut(weights[l] * grad_mix)
            grad_query = grad_query + dot3(weighted, buckets[l], NT)
            back_refs[l][i] = dot3(query_turned, weighted)
        along = jnp.sum(grad_query * query_normed, axis=-1, keepdims=True)
        grad_query = query_scale * (grad_query - query_normed * along)
        gq_ref[:, i * size : (i + 1) * size] = grad_query.astype(gq_ref.dtype)
    gl_ref[...] += grad_level
    gg_ref[...] += grad_gain


def back_kernel(
    base, k_ref, v_ref, beta_ref, cc_ref, cr_ref, t_ref, u_ref, dk_ref, du_ref, ds_ref,
    gk_ref, gv_ref, gb_ref,
):
    rows = k_ref.shape[0]
    size = dk_ref.shape[2]
    vsize = du_ref.shape[2]
    heads = du_ref.shape[0]
    t_ids, s_ids = coordinates(rows)
    strict = s_ids < t_ids

    @pl.when(pl.program_id(0) == 0)
    def _():
        gb_ref[...] = jnp.zeros_like(gb_ref)

    lanes = lax.broadcasted_iota(jnp.int32, gb_ref.shape, 1)
    grad_beta = jnp.zeros(gb_ref.shape, jnp.float32)
    for i in range(heads):
        head = base + pl.program_id(0) * heads + i
        key_float = k_ref[:, i * size : (i + 1) * size].astype(jnp.float32)
        value = v_ref[:, i * vsize : (i + 1) * vsize].astype(jnp.float32)
        gate = column(cc_ref[...], head)
        beta = column(beta_ref[...], head)
        gate_row = cr_ref[pl.ds(head, 1), :]
        key_scale = inverse_norm(key_float)
        key_normed = key_float * key_scale
        keys = cut(key_normed)
        pseudo = cut(u_ref[i])
        state = cut(ds_ref[i])
        trailing = jnp.exp(gate[rows - 1 :, :] - gate)
        grad_pseudo = du_ref[i] + trailing * dot3(keys, state)
        grad_key = dk_ref[i] + trailing * dot3(pseudo, state, NT)
        solved = dot3(cut(t_ref[i].T), cut(grad_pseudo))
        solved_parts = cut(solved)
        decay = decay_of(gate, gate_row, strict)
        grad_system = -dot3(solved_parts, pseudo, NT) * decay
        inner = dot3(keys, keys, NT)
        part = jnp.sum(solved * value, axis=-1, keepdims=True) + jnp.sum(
            grad_system * inner, axis=-1, keepdims=True
        )
        grad_beta = grad_beta + jnp.where(lanes == head, part, 0.0)
        grad_inner = beta * grad_system
        grad_key = grad_key + dot3(cut(grad_inner + grad_inner.T), keys)
        along = jnp.sum(grad_key * key_normed, axis=-1, keepdims=True)
        grad_key = key_scale * (grad_key - key_normed * along)
        gk_ref[:, i * size : (i + 1) * size] = grad_key.astype(gk_ref.dtype)
        gv_ref[:, i * vsize : (i + 1) * vsize] = (beta * solved).astype(gv_ref.dtype)
    gb_ref[...] += grad_beta


def local(query, key, value, beta, log_gate, level_weight, norm_gain, grad_out, grad_final_state):
    rows, heads, levels = level_weight.shape
    size = query.shape[1] // heads
    vsize = value.shape[1] // heads
    chunks = CHUNKS if heads % (CHUNKS * HEADS_STEP) == 0 else 1
    per = heads // chunks
    step = HEADS_STEP if per % HEADS_STEP == 0 else 1
    steps = per // step
    device = lax.axis_index("ctx")

    lower = jnp.tril(jnp.ones((rows, rows), jnp.float32))
    gates = lax.dot_general(lower, log_gate, NN, precision=topmost_level)
    gates_row = gates.T
    degrees = levels - 1
    top = degrees - 1
    half = 2**top
    unit = min(half, 2)
    hops = [[(half - unit + k, half + k) for k in range(unit)]]
    for stage in range(1, half // unit):
        hops.append(
            [(half + (stage - 1) * unit + k, half + stage * unit + k) for k in range(unit)]
        )

    offset = jnp.zeros((heads,), jnp.float32)
    group_total = gates[-1]
    uppers, offsets, own_sums, partner_sums = [], [], [], []
    for degree in range(degrees):
        is_upper = device >> degree & 1 == 1
        partner_total = from_partner(group_total, "ctx", degree)
        uppers.append(is_upper)
        offsets.append(offset)
        own_sums.append(group_total)
        partner_sums.append(partner_total)
        offset = jnp.where(is_upper, offset + partner_total, offset)
        group_total = group_total + partner_total
    factors = [jnp.ones((rows, heads), jnp.float32)]
    for degree in range(degrees):
        reach = jnp.where(uppers[degree], jnp.exp(offsets[degree]), 0.0)
        factors.append(jnp.exp(gates) * reach[None, :])
    factor = jnp.stack(factors, axis=2)
    weight = (level_weight * factor).reshape(rows, heads * levels)
    factor = factor.reshape(rows, heads * levels)

    def whole(array):
        return pl.BlockSpec(array.shape, lambda g: (0,) * array.ndim)

    def wide(chunk, width):
        return pl.BlockSpec((rows, step * width), lambda g: (0, chunk * steps + g))

    def tall(*dims):
        return pl.BlockSpec((step,) + dims, lambda g: (g, 0, 0))

    def fixed(*dims):
        return pl.BlockSpec(dims, lambda g: (0,) * len(dims))

    def floats(*dims):
        return jax.ShapeDtypeStruct(dims, jnp.float32)

    def call(kernel, name, in_specs, outs, out_specs, dots):
        return pl.pallas_call(
            kernel,
            name=name,
            grid=(steps,),
            in_specs=in_specs,
            out_specs=out_specs,
            out_shape=outs,
            compiler_params=pltpu.CompilerParams(vmem_limit_bytes=VMEM_LIMIT),
            cost_estimate=pl.CostEstimate(
                flops=per * dots * 6 * rows * rows * size * 4,
                bytes_accessed=per * rows * size * 4 * 8,
                transcendentals=per * rows * rows,
            ),
        )

    prepared = []
    for chunk in range(chunks):
        prepared.append(
            call(
                functools.partial(prepare_kernel, chunk * per),
                f"prepare{chunk}",
                [wide(chunk, size), wide(chunk, vsize), whole(beta), whole(gates), whole(gates_row)],
                (floats(per, rows, rows), floats(per, rows, vsize), floats(per, size, vsize)),
                (tall(rows, rows), tall(rows, vsize), tall(size, vsize)),
                16,
            )(key, value, beta, gates, gates_row)
        )

    def part_of(vector, chunk):
        return vector[chunk * per : (chunk + 1) * per][:, None, None]

    aggregates = [state for _, _, state in prepared]
    partners = [[None] * degrees for _ in range(chunks)]
    for degree in range(top):
        upper = uppers[degree]
        own_factor = jnp.where(upper, 1.0, jnp.exp(partner_sums[degree]))
        other_factor = jnp.where(upper, jnp.exp(own_sums[degree]), 1.0)
        for chunk in range(chunks):
            partner = from_partner(aggregates[chunk], "ctx", degree)
            partners[chunk][degree] = partner
            aggregates[chunk] = (
                part_of(own_factor, chunk) * aggregates[chunk]
                + part_of(other_factor, chunk) * partner
            )
    for chunk in range(chunks):
        passed = lax.ppermute(aggregates[chunk], "ctx", hops[0])
        gathered = passed
        for pairs in hops[1:]:
            passed = lax.ppermute(passed, "ctx", pairs)
            gathered = gathered + passed
        partners[chunk][top] = gathered

    rows_dev = grad_final_state.shape[0]
    own_start = device * rows_dev
    partner_start = (device ^ half) * rows_dev
    own_factor = jnp.where(uppers[top], 1.0, jnp.exp(partner_sums[top]))
    other_factor = jnp.where(uppers[top], jnp.exp(own_sums[top]), 1.0)

    def factor_rows(vector):
        spread = jnp.broadcast_to(vector[:, None], (heads, size)).reshape(heads * size, 1)
        return lax.dynamic_slice_in_dim(spread, own_start, rows_dev, 0)

    full_rows = jnp.concatenate(aggregates).reshape(heads * size, vsize)
    sent_rows = lax.dynamic_slice_in_dim(full_rows, partner_start, rows_dev, 0)
    own_rows = factor_rows(own_factor) * lax.dynamic_slice_in_dim(
        full_rows, own_start, rows_dev, 0
    ) + factor_rows(other_factor) * from_partner(sent_rows, "ctx", top)
    partner_seed = from_partner(grad_final_state, "ctx", top)
    seeds = jnp.zeros((heads * size, vsize), jnp.float32)
    seeds = lax.dynamic_update_slice_in_dim(seeds, grad_final_state, own_start, 0)
    seeds = lax.dynamic_update_slice_in_dim(seeds, partner_seed, partner_start, 0)
    seeds = own_factor[:, None, None] * seeds.reshape(heads, size, vsize)

    gain = norm_gain[None, :]
    finished = []
    for chunk in range(chunks):
        _, pseudo, _ = prepared[chunk]
        finished.append(
            call(
                functools.partial(finish_kernel, chunk * per, levels),
                f"finish{chunk}",
                [wide(chunk, size), wide(chunk, size), wide(chunk, vsize), tall(rows, vsize)]
                + [whole(gates), whole(gates_row), whole(weight), whole(factor), whole(gain)]
                + [tall(size, vsize)] * degrees,
                (
                    jax.ShapeDtypeStruct((rows, per * size), jnp.bfloat16),
                    floats(per, rows, size),
                    floats(per, rows, vsize),
                    floats(rows, heads * levels),
                    floats(1, vsize),
                )
                + (floats(per, size, vsize),) * degrees,
                (
                    wide(0, size),
                    tall(rows, size),
                    tall(rows, vsize),
                    fixed(rows, heads * levels),
                    fixed(1, vsize),
                )
                + (tall(size, vsize),) * degrees,
                6 + 3 * degrees,
            )(
                query, key, grad_out, pseudo, gates, gates_row, weight, factor, gain,
                *partners[chunk],
            )
        )
    grad_gain = sum(result[4] for result in finished)[0]
    for degree in range(degrees):
        grad_gain = grad_gain + from_partner(grad_gain, "ctx", degree)

    adjoints = []
    for chunk in range(chunks):
        carried = finished[chunk][5 + top]
        for pairs in reversed(hops[1:]):
            back_pairs = [(target, source) for source, target in pairs]
            carried = carried + lax.ppermute(carried, "ctx", back_pairs)
        back_pairs = [(target, source) for source, target in hops[0]]
        carried = lax.ppermute(carried, "ctx", back_pairs)
        adjoints.append(seeds[chunk * per : (chunk + 1) * per] + carried)
    for degree in reversed(range(top)):
        upper = uppers[degree]
        send_factor = jnp.where(upper, jnp.exp(own_sums[degree]), 1.0)
        keep_factor = jnp.where(upper, 1.0, jnp.exp(partner_sums[degree]))
        for chunk in range(chunks):
            adjoint = adjoints[chunk]
            outgoing = finished[chunk][5 + degree] + part_of(send_factor, chunk) * adjoint
            incoming = from_partner(outgoing, "ctx", degree)
            adjoints[chunk] = part_of(keep_factor, chunk) * adjoint + incoming

    backs = []
    for chunk in range(chunks):
        inverse, pseudo, _ = prepared[chunk]
        grad_key, grad_pseudo = finished[chunk][1:3]
        backs.append(
            call(
                functools.partial(back_kernel, chunk * per),
                f"back{chunk}",
                [wide(chunk, size), wide(chunk, vsize), whole(beta), whole(gates), whole(gates_row)]
                + [tall(rows, rows), tall(rows, vsize), tall(rows, size), tall(rows, vsize)]
                + [tall(size, vsize)],
                (
                    jax.ShapeDtypeStruct((rows, per * size), jnp.bfloat16),
                    jax.ShapeDtypeStruct((rows, per * vsize), jnp.bfloat16),
                    floats(rows, heads),
                ),
                (wide(0, size), wide(0, vsize), fixed(rows, heads)),
                6,
            )(
                key, value, beta, gates, gates_row, inverse, pseudo, grad_key, grad_pseudo,
                adjoints[chunk],
            )
        )
    return (
        jnp.concatenate([result[0] for result in finished], axis=1),
        jnp.concatenate([result[0] for result in backs], axis=1),
        jnp.concatenate([result[1] for result in backs], axis=1),
        sum(result[2] for result in backs),
        sum(result[3] for result in finished).reshape(rows, heads, levels),
        grad_gain,
        own_rows,
    )


def solution(mesh):
    in_specs = (
        P(("rep", "ctx"), None),
        P(("rep", "ctx"), None),
        P(("rep", "ctx"), None),
        P(("rep", "ctx"), None),
        P(("rep", "ctx"), None),
        P(("rep", "ctx"), None, None),
        P(),
        P(("rep", "ctx"), None),
        P(("rep", "ctx"), None),
    )
    out_specs = (
        P(("rep", "ctx"), None),
        P(("rep", "ctx"), None),
        P(("rep", "ctx"), None),
        P(("rep", "ctx"), None),
        P(("rep", "ctx"), None, None),
        P("rep"),
        P(("rep", "ctx"), None),
    )
    return jax.shard_map(local, mesh=mesh, in_specs=in_specs, out_specs=out_specs, check_vma=False)
```
